32 devices in a mesh: groups: 2 (over y), row: 4 (over z), col: 4 (over x, core), depth: 1.
Axes of the slice: x: 2, y: 2, z: 4, core: 2. Of those that a mesh axis runs over, the one named last changes fastest.
Arguments:
- mantissa: bfloat16 [1024, 8192], P(('groups', 'row', 'col'), 'depth'), parts along dimension 0, may hold values from -0.0625 to 0.0625
- exponent: int32 [1024], P(('groups', 'row', 'col')), parts along dimension 0, may hold values from -2 to 2
Outputs:
- kernel_gram: float32 [1024, 512], P(('groups', 'row'), ('col', 'depth')), parts along dimension 0
The draws below stay inside these ranges and needn't reach their ends.
There are 2 independent parts, one for each index of `groups`. The reference program is written for one: setup_inputs(seed, part) draws one part's arguments, and reference() takes and returns one part's arrays. A program takes and returns all parts, laid end to end along the dimension named above; each array names one. Nothing has to cross between parts.
All inputs are finite; a program needn't handle non-finite values.
Results may differ from the reference program's by a relative error of at most 0.0003.
Values may be sent and summed in bfloat16 or wider, within the bound.
A program may use at most 64 MiB of HBM per device.

```python
import jax
import jax.numpy as jnp
from jax import lax

F = 8192
EX = 512


def with_ends(array, stream_key, smallest, largest):
    extent = array.shape
    index_at = [jax.random.randint(jax.random.fold_in(stream_key, axis), (), 0, extent[axis]) for axis in range(len(extent))]
    array = array.at[tuple(index_at)].set(smallest)
    longest = extent.index(max(extent))
    index_at[longest] = (index_at[longest] + 1) % extent[longest]
    return array.at[tuple(index_at)].set(largest)


def shard_levels(key, extent, split, low, high):
    factor_of = 1.0
    for position, shards_of in split:
        steps = jax.random.uniform(jax.random.fold_in(jax.random.fold_in(key, 6), position), (shards_of,), jnp.float32, low / len(split), high / len(split))
        factor_of = factor_of * jnp.repeat(jnp.exp(steps), extent[position] // shards_of).reshape((-1,) + (1,) * (len(extent) - 1 - position))
    return factor_of


def centred(stream_key, extent, scale, bound, cuts=(), held_as=jnp.bfloat16):
    array = scale * jax.random.normal(stream_key, extent, jnp.float32)
    if cuts:
        array = array * shard_levels(stream_key, extent, cuts, -0.22, 0.18)
    return jnp.clip(array, -bound, bound).astype(held_as)


def setup_inputs(seed: int = 0, part: int = 0) -> dict:
    arg_keys = jax.random.split(jax.random.key(seed), 3)
    part_splits = jax.random.split(jax.random.fold_in(arg_keys[2], part), 3)
    mantissa = centred(part_splits[0], (EX, F), F ** -0.5, 0.0625, ((0, 16),))
    exponent = with_ends(jax.random.randint(part_splits[1], (EX,), -2, 3), jax.random.fold_in(part_splits[1], 1), -2, 2).astype(jnp.int32)
    return dict(mantissa=mantissa, exponent=exponent)


def reference(mantissa, exponent):
    scales = jnp.exp2(exponent.astype(jnp.float32))
    features = (mantissa.astype(jnp.float32) * scales[:, None]).astype(jnp.bfloat16)
    wide = features.astype(jnp.float32)
    return jnp.dot(wide, wide.T, precision=lax.Precision.HIGHEST)
```

```python
import functools

import jax
import jax.numpy as jnp
from jax import lax
from jax.experimental import pallas as pl
from jax.experimental.pallas import tpu as pltpu
from jax.sharding import PartitionSpec as P

CHUNKS = 4
MESH = pl.DeviceIdType.MESH


def held_upper(rows, z, b):
    ordinary = (b >= 1) & (b <= z) & jnp.logical_not((z == rows - 1) & (b == 1))
    return ordinary | ((z == rows - 2) & (b == rows - 1))


def held_lower(rows, z, b):
    return held_upper(rows, rows - 1 - z, b)


def worked(rows, z, b):
    return held_upper(rows, z, b) | held_lower(rows, z, rows - b)


def scale_of(exponent):
    size = jnp.abs(exponent)
    up = jnp.ones(exponent.shape, jnp.float32)
    down = up
    for bit in range(7):
        is_set = ((size >> bit) & 1) == 1
        up = jnp.where(is_set, up * 2.0 ** (2**bit), up)
        down = jnp.where(is_set, down * 2.0 ** -(2**bit), down)
    return jnp.where(exponent < 0, down, up)


def kernel(rows, cols, depths, mantissa, exponent, out, raw, tile, upper, lower, acc_a, acc_b, sums, direct, mirror,
           load_sem, plane_send, plane_recv, up_send, up_recv, down_send, down_recv, extra_send,
           direct_send, direct_recv, mirror_send, mirror_recv):
    z, c, d = lax.axis_index("row"), lax.axis_index("col"), lax.axis_index("depth")
    n, features = raw.shape
    size = n * cols
    half = features // 2
    width = half // CHUNKS
    q = c * depths + d

    load = pltpu.make_async_copy(mantissa, raw, load_sem)
    load.start()

    barrier = pltpu.get_barrier_semaphore()

    def greet(k, _):
        there = {"row": k // (cols * depths), "col": (k // depths) % cols, "depth": k % depths}

        @pl.when(k != z * cols * depths + q)
        def _():
            pl.semaphore_signal(barrier, inc=1, device_id=there, device_id_type=MESH)

        return 0

    lax.fori_loop(0, rows * cols * depths, greet, 0)

    wide = jnp.broadcast_to(exponent[...].reshape(1, n), (n, n))
    eye = lax.broadcasted_iota(jnp.int32, (n, n), 0) == lax.broadcasted_iota(jnp.int32, (n, n), 1)
    scale = scale_of(jnp.sum(jnp.where(eye, wide, 0), axis=1, keepdims=True))
    load.wait()
    own_rows = pl.ds(pl.multiple_of(c * n, n), n)
    for i in range(2 * CHUNKS):
        piece = pl.ds(i * width, width)
        scaled = (raw[:, piece].astype(jnp.float32) * scale).astype(jnp.bfloat16)
        tile[own_rows, piece] = scaled
        if i < CHUNKS:
            upper[pl.ds(0, n), piece] = scaled
        else:
            lower[pl.ds(0, n), pl.ds((i - CHUNKS) * width, width)] = scaled
    pl.semaphore_wait(barrier, rows * cols * depths - 1)

    def plane_copy(rel, bit, chunk):
        block = tile.at[pl.ds(pl.multiple_of((c ^ rel) * n, n), n), pl.ds(chunk * width, width)]
        return pltpu.make_async_remote_copy(
            src_ref=block, dst_ref=block, send_sem=plane_send.at[rel | bit, chunk],
            recv_sem=plane_recv.at[rel | bit, chunk], device_id={"col": c ^ bit}, device_id_type=MESH)

    def lower_bits(rel):
        bit = (rel & -rel if rel else cols) >> 1
        while bit:
            yield bit
            bit >>= 1

    def plane_start(rel, chunk):
        for bit in lower_bits(rel):
            plane_copy(rel, bit, chunk).start()

    def plane_arrived(rel, chunk):
        block = tile.at[pl.ds(pl.multiple_of((c ^ rel) * n, n), n), pl.ds(chunk * width, width)]
        pltpu.make_async_copy(block, block, plane_recv.at[rel, chunk]).wait()

    def line_copy(buffer, send, recv, there, b, i):
        piece = pl.ds(i * width, width)
        return pltpu.make_async_remote_copy(
            src_ref=buffer.at[pl.ds(b * n, n), piece], dst_ref=buffer.at[pl.ds((b + 1) * n, n), piece],
            send_sem=send.at[b, i], recv_sem=recv.at[b + 1, i], device_id={"row": there}, device_id_type=MESH)

    def extra_copy(buffer, recv, there, i):
        piece = pl.ds(i * width, width)
        return pltpu.make_async_remote_copy(
            src_ref=buffer.at[pl.ds(0, n), piece], dst_ref=buffer.at[pl.ds((rows - 1) * n, n), piece],
            send_sem=extra_send.at[i], recv_sem=recv.at[rows - 1, i], device_id={"row": there}, device_id_type=MESH)

    def line_arrived(buffer, recv, b, i):
        block = buffer.at[pl.ds(b * n, n), pl.ds(i * width, width)]
        pltpu.make_async_copy(block, block, recv.at[b, i]).wait()

    m = rows - 1 - z
    for i in range(CHUNKS):
        @pl.when(z < rows - 2)
        def _():
            line_copy(upper, up_send, up_recv, z + 1, 0, i).start()

        @pl.when(z > 1)
        def _():
            line_copy(lower, down_send, down_recv, z - 1, 0, i).start()

        plane_start(0, i)
        plane_start(0, CHUNKS + i)

    for i in range(CHUNKS):
        @pl.when(z == 0)
        def _():
            line_copy(upper, up_send, up_recv, z + 1, 0, i).wait_send()
            extra_copy(lower, down_recv, z + 1, i).start()

        @pl.when(z == rows - 1)
        def _():
            line_copy(lower, down_send, down_recv, z - 1, 0, i).wait_send()
            extra_copy(upper, up_recv, z - 1, i).start()

    def arrive(b, i):
        @pl.when(held_upper(rows, z, b))
        def _():
            line_arrived(upper, up_recv, b, i)

        @pl.when(held_lower(rows, z, b))
        def _():
            line_arrived(lower, down_recv, b, i)

        if b < rows - 1:
            @pl.when((b <= z) & (z < rows - 1))
            def _():
                line_copy(upper, up_send, up_recv, z + 1, b, i).start()

            @pl.when((b <= m) & (m < rows - 1))
            def _():
                line_copy(lower, down_send, down_recv, z - 1, b, i).start()

    def plane_arrive(chunk):
        for bit in reversed(range(cols.bit_length() - 1)):
            for rel in range(1 << bit, cols, 1 << (bit + 1)):
                plane_arrived(rel, chunk)
                plane_start(rel, chunk)

    for b in range(1, rows - 2):
        for i in range(CHUNKS):
            arrive(b, i)
            if b == rows - 3 and i % 2 == 1:
                plane_arrive(i // 2)
                plane_arrive(CHUNKS + i // 2)

    dims = (((1,), (1,)), ((), ()))
    for i in range(CHUNKS):
        arrive(rows - 2, i)
        if i >= CHUNKS // 2:
            plane_arrive(i)
            plane_arrive(CHUNKS + i)
        arrive(rows - 1, i)
        piece, other = pl.ds(i * width, width), pl.ds(half + i * width, width)
        term_a = lax.dot_general(upper[:, piece], tile[:, piece], dims, preferred_element_type=jnp.float32)
        term_b = lax.dot_general(lower[:, piece], tile[:, other], dims, preferred_element_type=jnp.float32)
        if i == 0:
            acc_a[...] = term_a
            acc_b[...] = term_b
        else:
            acc_a[...] += term_a
            acc_b[...] += term_b

    def place(row, tile_index):
        return {"row": row, "col": tile_index // depths, "depth": tile_index % depths}

    stripe = pl.ds(pl.multiple_of(c * n, n), n)

    def direct_copy(b, j):
        return pltpu.make_async_remote_copy(
            src_ref=sums.at[b], dst_ref=direct.at[d, stripe], send_sem=direct_send.at[b],
            recv_sem=direct_recv.at[d, c], device_id=place(z, j), device_id_type=MESH)

    def mirror_copy(b, j):
        return pltpu.make_async_remote_copy(
            src_ref=sums.at[b], dst_ref=mirror.at[d, stripe], send_sem=mirror_send.at[b],
            recv_sem=mirror_recv.at[d, c], device_id=place(j, z), device_id_type=MESH)

    for b in range(1, rows):
        j = lax.rem(z - b + rows, rows)

        @pl.when(worked(rows, z, b))
        def _():
            first = jnp.where(held_upper(rows, z, b), acc_a[pl.ds(b * n, n), :], 0.0)
            second = jnp.where(held_lower(rows, z, rows - b), acc_b[pl.ds((rows - b) * n, n), :], 0.0)
            sums[b] = first + second
            mirror_copy(b, j).start()

            @pl.when(j != q)
            def _():
                direct_copy(b, j).start()

            @pl.when(j == q)
            def _():
                direct[d, stripe] = sums[b]

    sums[0] = acc_a[pl.ds(0, n), :] + acc_b[pl.ds(0, n), :]

    @pl.when(z != q)
    def _():
        mirror_copy(0, z).start()

    @pl.when(z == q)
    def _():
        mirror[d, stripe] = sums[0]

    for b in range(rows):
        for i in range(CHUNKS):
            if b < rows - 1:
                @pl.when((b <= z) & (z < rows - 1) & jnp.logical_not((b == 0) & ((z == rows - 2) | (z == 0))))
                def _():
                    line_copy(upper, up_send, up_recv, z + 1, b, i).wait_send()

                @pl.when((b <= m) & (m < rows - 1) & jnp.logical_not((b == 0) & ((m == rows - 2) | (m == 0))))
                def _():
                    line_copy(lower, down_send, down_recv, z - 1, b, i).wait_send()

    for i in range(CHUNKS):
        @pl.when((z == 0) | (z == rows - 1))
        def _():
            extra_copy(lower, down_recv, 1, i).wait_send()

    for chunk in range(2 * CHUNKS):
        for rel in range(cols):
            for bit in lower_bits(rel):
                plane_copy(rel, bit, chunk).wait_send()

    def wait_block(buffer, recv, cc, dd):
        block = buffer.at[dd, pl.ds(cc * n, n)]
        pltpu.make_async_copy(block, block, recv.at[dd, cc]).wait()

    has_direct = (z != q) & worked(rows, z, lax.rem(z - q + rows, rows))
    has_mirror = (z == q) | worked(rows, q, lax.rem(q - z + rows, rows))

    def gathered(buffer):
        total = buffer[0]
        for dd in range(1, depths):
            total = total + buffer[dd]
        return total

    @pl.when(has_direct)
    def _():
        for dd in range(depths):
            for cc in range(cols):
                @pl.when((cc != c) | (dd != d))
                def _():
                    wait_block(direct, direct_recv, cc, dd)

        out[...] = gathered(direct).T

    @pl.when(has_mirror)
    def _():
        for dd in range(depths):
            for cc in range(cols):
                @pl.when((z != q) | (cc != c) | (dd != d))
                def _():
                    wait_block(mirror, mirror_recv, cc, dd)

        total = gathered(mirror)

        @pl.when(has_direct)
        def _():
            out[...] += total

        @pl.when(jnp.logical_not(has_direct))
        def _():
            out[...] = total

    for b in range(rows):
        j = lax.rem(z - b + rows, rows)
        if b:
            @pl.when(worked(rows, z, b))
            def _():
                mirror_copy(b, j).wait_send()

                @pl.when(j != q)
                def _():
                    direct_copy(b, j).wait_send()
        else:
            @pl.when(z != q)
            def _():
                mirror_copy(0, z).wait_send()


def shards(rows, cols, depths, mantissa, exponent):
    n, features = mantissa.shape
    size = n * cols
    half = features // 2
    dma = pltpu.SemaphoreType.DMA
    return pl.pallas_call(
        functools.partial(kernel, rows, cols, depths),
        out_shape=jax.ShapeDtypeStruct((size, size), jnp.float32),
        in_specs=[pl.BlockSpec(memory_space=pl.ANY), pl.BlockSpec(memory_space=pltpu.VMEM)],
        out_specs=pl.BlockSpec(memory_space=pltpu.VMEM),
        scratch_shapes=[
            pltpu.VMEM((n, features), jnp.bfloat16),
            pltpu.VMEM((size, features), jnp.bfloat16),
            pltpu.VMEM((rows * n, half), jnp.bfloat16),
            pltpu.VMEM((rows * n, half), jnp.bfloat16),
            pltpu.VMEM((rows * n, size), jnp.float32),
            pltpu.VMEM((rows * n, size), jnp.float32),
            pltpu.VMEM((rows, n, size), jnp.float32),
            pltpu.VMEM((depths, size, size), jnp.float32),
            pltpu.VMEM((depths, size, size), jnp.float32),
            dma,
            dma((cols, 2 * CHUNKS)), dma((cols, 2 * CHUNKS)),
            dma((rows, CHUNKS)), dma((rows, CHUNKS)),
            dma((rows, CHUNKS)), dma((rows, CHUNKS)),
            dma((CHUNKS,)),
            dma((rows,)), dma((depths, cols)),
            dma((rows,)), dma((depths, cols)),
        ],
        compiler_params=pltpu.CompilerParams(
            collective_id=0, has_side_effects=True, vmem_limit_bytes=48 * 2**20),
    )(mantissa, exponent)


def solution(mesh):
    rows, cols, depths = (mesh.shape[axis] for axis in ("row", "col", "depth"))
    assert rows >= 3 and cols & (cols - 1) == 0 and rows == cols * depths
    in_specs = (P(("groups", "row", "col"), "depth"), P(("groups", "row", "col")))
    out_specs = P(("groups", "row"), ("col", "depth"))
    return jax.shard_map(
        functools.partial(shards, rows, cols, depths), mesh=mesh, in_specs=in_specs, out_specs=out_specs, check_vma=False)
```

```python
import functools

import jax
import jax.numpy as jnp
from jax import lax
from jax.experimental import pallas as pl
from jax.experimental.pallas import tpu as pltpu
from jax.sharding import PartitionSpec as P

CHUNKS = 4
PLANE = 2
LAG = 3
MESH = pl.DeviceIdType.MESH


def held_upper(rows, z, b):
    ordinary = (b >= 1) & (b <= z) & jnp.logical_not((z == rows - 1) & (b == 1))
    return ordinary | ((z == rows - 2) & (b == rows - 1))


def held_lower(rows, z, b):
    return held_upper(rows, rows - 1 - z, b)


def worked(rows, z, b):
    return held_upper(rows, z, b) | held_lower(rows, z, rows - b)


def scale_of(exponent):
    size = jnp.abs(exponent)
    up = jnp.ones(exponent.shape, jnp.float32)
    down = up
    for bit in range(7):
        is_set = ((size >> bit) & 1) == 1
        up = jnp.where(is_set, up * 2.0 ** (2**bit), up)
        down = jnp.where(is_set, down * 2.0 ** -(2**bit), down)
    return jnp.where(exponent < 0, down, up)


def kernel(rows, cols, depths, mantissa, exponent, out, raw, powers, tile, upper, lower, acc_a, acc_b, sums, direct, mirror,
           load_sem, power_sem, plane_send, plane_recv, up_send, up_recv, down_send, down_recv, extra_send,
           direct_send, direct_recv, mirror_send, mirror_recv):
    z, c, d = lax.axis_index("row"), lax.axis_index("col"), lax.axis_index("depth")
    n, features = raw.shape
    size = n * cols
    half = features // 2
    width = half // CHUNKS
    q = c * depths + d

    def load(half_index, i):
        piece = pl.ds(half_index * half + i * width, width)
        return pltpu.make_async_copy(mantissa.at[:, piece], raw.at[:, piece], load_sem.at[half_index, i])

    for i in range(CHUNKS):
        for half_index in range(2):
            load(half_index, i).start()
    load_powers = pltpu.make_async_copy(exponent, powers, power_sem)
    load_powers.start()

    barrier = pltpu.get_barrier_semaphore()

    def greet(k, _):
        @pl.when(k != q)
        def _():
            there = {"col": k // depths, "depth": k % depths}
            pl.semaphore_signal(barrier, inc=1, device_id=there, device_id_type=MESH)

        return 0

    lax.fori_loop(0, cols * depths, greet, 0)

    @pl.when(z > 0)
    def _():
        pl.semaphore_signal(barrier, inc=1, device_id={"row": z - 1}, device_id_type=MESH)

    @pl.when(z < rows - 1)
    def _():
        pl.semaphore_signal(barrier, inc=1, device_id={"row": z + 1}, device_id_type=MESH)

    load_powers.wait()
    wide = jnp.broadcast_to(powers[...].reshape(1, n), (n, n))
    eye = lax.broadcasted_iota(jnp.int32, (n, n), 0) == lax.broadcasted_iota(jnp.int32, (n, n), 1)
    scale = scale_of(jnp.sum(jnp.where(eye, wide, 0), axis=1, keepdims=True))
    own_rows = pl.ds(pl.multiple_of(c * n, n), n)

    def scaled(half_index, i, block):
        load(half_index, i).wait()
        piece = pl.ds(half_index * half + i * width, width)
        value = (raw[:, piece].astype(jnp.float32) * scale).astype(jnp.bfloat16)
        tile[own_rows, piece] = value
        block[pl.ds(0, n), pl.ds(i * width, width)] = value

    span = half // PLANE

    def plane_block(rel, t):
        start = t % 2 * half + t // 2 * span
        return tile.at[pl.ds(pl.multiple_of((c ^ rel) * n, n), n), pl.ds(start, span)]

    def plane_copy(rel, bit, t):
        block = plane_block(rel, t)
        return pltpu.make_async_remote_copy(
            src_ref=block, dst_ref=block, send_sem=plane_send.at[rel | bit],
            recv_sem=plane_recv.at[rel | bit, t], device_id={"col": c ^ bit}, device_id_type=MESH)

    def lower_bits(rel):
        bit = (rel & -rel if rel else cols) >> 1
        while bit:
            yield bit
            bit >>= 1

    def plane_arrivals(t):
        for bit in reversed(range(cols.bit_length() - 1)):
            for rel in range(1 << bit, cols, 1 << (bit + 1)):
                block = plane_block(rel, t)
                pltpu.make_async_copy(block, block, plane_recv.at[rel, t]).wait()
                for low in lower_bits(rel):
                    plane_copy(rel, low, t).start()

    def line_copy(buffer, send, recv, there, b, i):
        piece = pl.ds(i * width, width)
        return pltpu.make_async_remote_copy(
            src_ref=buffer.at[pl.ds(b * n, n), piece], dst_ref=buffer.at[pl.ds((b + 1) * n, n), piece],
            send_sem=send.at[b], recv_sem=recv.at[b + 1, i], device_id={"row": there}, device_id_type=MESH)

    def extra_copy(buffer, recv, there, i):
        piece = pl.ds(i * width, width)
        return pltpu.make_async_remote_copy(
            src_ref=buffer.at[pl.ds(0, n), piece], dst_ref=buffer.at[pl.ds((rows - 1) * n, n), piece],
            send_sem=extra_send, recv_sem=recv.at[rows - 1, i], device_id={"row": there}, device_id_type=MESH)

    def line_arrived(buffer, recv, b, i):
        block = buffer.at[pl.ds(b * n, n), pl.ds(i * width, width)]
        pltpu.make_async_copy(block, block, recv.at[b, i]).wait()

    m = rows - 1 - z

    def line_sends(t):
        b, i = divmod(t, CHUNKS)

        @pl.when((z < rows - 2) & (b <= z))
        def _():
            line_copy(upper, up_send, up_recv, z + 1, b, i).start()

        @pl.when((m < rows - 2) & (b <= m))
        def _():
            line_copy(lower, down_send, down_recv, z - 1, b, i).start()

        if b == 1:
            @pl.when(z == 0)
            def _():
                extra_copy(lower, down_recv, z + 1, i).start()

            @pl.when(m == 0)
            def _():
                extra_copy(upper, up_recv, z - 1, i).start()

    def line_arrivals(t):
        b, i = divmod(t, CHUNKS)
        b += 1

        @pl.when((b <= z) & (z <= rows - 2))
        def _():
            line_arrived(upper, up_recv, b, i)

            @pl.when(z == rows - 2)
            def _():
                line_copy(upper, up_send, up_recv, z + 1, b, i).start()

        @pl.when((b <= m) & (m <= rows - 2))
        def _():
            line_arrived(lower, down_recv, b, i)

            @pl.when(m == rows - 2)
            def _():
                line_copy(lower, down_send, down_recv, z - 1, b, i).start()

    def last_arrivals(i):
        @pl.when(z == rows - 2)
        def _():
            line_arrived(upper, up_recv, rows - 1, i)

        @pl.when(m == rows - 2)
        def _():
            line_arrived(lower, down_recv, rows - 1, i)

        @pl.when(z == rows - 1)
        def _():
            for b in range(2, rows):
                line_arrived(upper, up_recv, b, i)

        @pl.when(m == rows - 1)
        def _():
            for b in range(2, rows):
                line_arrived(lower, down_recv, b, i)

    dims = (((1,), (1,)), ((), ()))

    def multiply(i):
        piece, other = pl.ds(i * width, width), pl.ds(half + i * width, width)
        term_a = lax.dot_general(upper[:, piece], tile[:, piece], dims, preferred_element_type=jnp.float32)
        term_b = lax.dot_general(lower[:, piece], tile[:, other], dims, preferred_element_type=jnp.float32)
        if i == 0:
            acc_a[...] = term_a
            acc_b[...] = term_b
        else:
            acc_a[...] += term_a
            acc_b[...] += term_b

    line_steps = (rows - 2) * CHUNKS
    plane_done = 0
    for step in range(line_steps + LAG):
        if step < CHUNKS:
            scaled(0, step, upper)
            scaled(1, step, lower)
        if step == 0:
            pl.semaphore_wait(barrier, cols * depths + 1 - jnp.where((z == 0) | (z == rows - 1), 1, 0))
        if step < line_steps:
            line_sends(step)
        per_span = CHUNKS // PLANE
        if step < CHUNKS and step % per_span == per_span - 1:
            for t in (step // per_span * 2, step // per_span * 2 + 1):
                for bit in lower_bits(0):
                    plane_copy(0, bit, t).start()
        done = step - LAG
        if done >= 0:
            line_arrivals(done)
            i = done - (rows - 3) * CHUNKS
            due = min((done + 1) // per_span, 2 * PLANE)
            if i >= 0:
                due = max(due, i // per_span * 2 + 2)
            for t in range(plane_done, due):
                plane_arrivals(t)
            plane_done = due
            if i >= 0:
                last_arrivals(i)
                multiply(i)

    def place(row, tile_index):
        return {"row": row, "col": tile_index // depths, "depth": tile_index % depths}

    stripe = pl.ds(pl.multiple_of(c * n, n), n)

    def direct_copy(b, j):
        return pltpu.make_async_remote_copy(
            src_ref=sums.at[b], dst_ref=direct.at[d, stripe], send_sem=direct_send.at[b],
            recv_sem=direct_recv, device_id=place(z, j), device_id_type=MESH)

    def mirror_copy(b, j):
        return pltpu.make_async_remote_copy(
            src_ref=sums.at[b], dst_ref=mirror.at[d, stripe], send_sem=mirror_send.at[b],
            recv_sem=mirror_recv, device_id=place(j, z), device_id_type=MESH)

    for b in range(1, rows):
        j = lax.rem(z - b + rows, rows)

        @pl.when(worked(rows, z, b))
        def _():
            first = jnp.where(held_upper(rows, z, b), acc_a[pl.ds(b * n, n), :], 0.0)
            second = jnp.where(held_lower(rows, z, rows - b), acc_b[pl.ds((rows - b) * n, n), :], 0.0)
            sums[b] = first + second
            mirror_copy(b, j).start()

            @pl.when(j != q)
            def _():
                direct_copy(b, j).start()

            @pl.when(j == q)
            def _():
                direct[d, stripe] = sums[b]

    sums[0] = acc_a[pl.ds(0, n), :] + acc_b[pl.ds(0, n), :]

    @pl.when(z != q)
    def _():
        mirror_copy(0, z).start()

    @pl.when(z == q)
    def _():
        mirror[d, stripe] = sums[0]

    def sent(block, sem):
        pltpu.make_async_copy(block, block, sem).wait()

    for b in range(rows - 1):
        @pl.when((b <= z) & (z < rows - 1) & jnp.logical_not((b == 0) & (z == rows - 2)))
        def _():
            sent(upper.at[pl.ds(b * n, n)], up_send.at[b])

        @pl.when((b <= m) & (m < rows - 1) & jnp.logical_not((b == 0) & (m == rows - 2)))
        def _():
            sent(lower.at[pl.ds(b * n, n)], down_send.at[b])

    @pl.when((z == 0) | (m == 0))
    def _():
        sent(upper.at[pl.ds(0, n)], extra_send)

    for rel in range(1, cols):
        sent(tile.at[own_rows], plane_send.at[rel])

    def received(buffer, recv, own):
        @pl.when(own)
        def _():
            others = sums.at[pl.ds(0, cols * depths - 1)]
            pltpu.make_async_copy(others, others, recv).wait()

        @pl.when(jnp.logical_not(own))
        def _():
            pltpu.make_async_copy(buffer, buffer, recv).wait()

    has_direct = (z != q) & worked(rows, z, lax.rem(z - q + rows, rows))
    has_mirror = (z == q) | worked(rows, q, lax.rem(q - z + rows, rows))

    def gathered(buffer):
        total = buffer[0]
        for dd in range(1, depths):
            total = total + buffer[dd]
        return total

    @pl.when(has_direct)
    def _():
        others = sums.at[pl.ds(0, cols * depths - 1)]
        pltpu.make_async_copy(others, others, direct_recv).wait()
        out[...] = gathered(direct).T

    @pl.when(has_mirror)
    def _():
        received(mirror, mirror_recv, z == q)
        total = gathered(mirror)

        @pl.when(has_direct)
        def _():
            out[...] += total

        @pl.when(jnp.logical_not(has_direct))
        def _():
            out[...] = total

    for b in range(rows):
        j = lax.rem(z - b + rows, rows)
        if b:
            @pl.when(worked(rows, z, b))
            def _():
                mirror_copy(b, j).wait_send()

                @pl.when(j != q)
                def _():
                    direct_copy(b, j).wait_send()
        else:
            @pl.when(z != q)
            def _():
                mirror_copy(0, z).wait_send()


def shards(rows, cols, depths, mantissa, exponent):
    n, features = mantissa.shape
    size = n * cols
    half = features // 2
    dma = pltpu.SemaphoreType.DMA
    return pl.pallas_call(
        functools.partial(kernel, rows, cols, depths),
        out_shape=jax.ShapeDtypeStruct((size, size), jnp.float32),
        in_specs=[pl.BlockSpec(memory_space=pltpu.HBM)] * 2,
        out_specs=pl.BlockSpec(memory_space=pltpu.VMEM),
        scratch_shapes=[
            pltpu.VMEM((n, features), jnp.bfloat16),
            pltpu.VMEM((n,), jnp.int32),
            pltpu.VMEM((size, features), jnp.bfloat16),
            pltpu.VMEM((rows * n, half), jnp.bfloat16),
            pltpu.VMEM((rows * n, half), jnp.bfloat16),
            pltpu.VMEM((rows * n, size), jnp.float32),
            pltpu.VMEM((rows * n, size), jnp.float32),
            pltpu.VMEM((rows, n, size), jnp.float32),
            pltpu.VMEM((depths, size, size), jnp.float32),
            pltpu.VMEM((depths, size, size), jnp.float32),
            dma((2, CHUNKS)), dma,
            dma((cols,)), dma((cols, 2 * PLANE)),
            dma((rows,)), dma((rows, CHUNKS)),
            dma((rows,)), dma((rows, CHUNKS)),
            dma,
            dma((rows,)), dma,
            dma((rows,)), dma,
        ],
        compiler_params=pltpu.CompilerParams(
            collective_id=0, has_side_effects=True, vmem_limit_bytes=63 * 2**20),
    )(mantissa, exponent)


def solution(mesh):
    rows, cols, depths = (mesh.shape[axis] for axis in ("row", "col", "depth"))
    assert rows >= 4 and cols & (cols - 1) == 0 and rows == cols * depths
    in_specs = (P(("groups", "row", "col"), "depth"), P(("groups", "row", "col")))
    out_specs = P(("groups", "row"), ("col", "depth"))
    return jax.shard_map(
        functools.partial(shards, rows, cols, depths), mesh=mesh, in_specs=in_specs, out_specs=out_specs, check_vma=False)
```

```python
import functools

import jax
import jax.numpy as jnp
from jax import lax
from jax.experimental import pallas as pl
from jax.experimental.pallas import tpu as pltpu
from jax.sharding import PartitionSpec as P

PIECES = (4, 4, 4, 4)
CHUNKS = len(PIECES)
PLANE = 2
LAG = 3
MESH = pl.DeviceIdType.MESH


def held_upper(rows, z, b):
    ordinary = (b >= 1) & (b <= z) & jnp.logical_not((z == rows - 1) & (b == 1))
    return ordinary | ((z == rows - 2) & (b == rows - 1))


def held_lower(rows, z, b):
    return held_upper(rows, rows - 1 - z, b)


def worked(rows, z, b):
    return held_upper(rows, z, b) | held_lower(rows, z, rows - b)


def scale_of(exponent):
    size = jnp.abs(exponent)
    up = jnp.ones(exponent.shape, jnp.float32)
    down = up
    for bit in range(7):
        is_set = ((size >> bit) & 1) == 1
        up = jnp.where(is_set, up * 2.0 ** (2**bit), up)
        down = jnp.where(is_set, down * 2.0 ** -(2**bit), down)
    return jnp.where(exponent < 0, down, up)


def kernel(rows, cols, depths, mantissa, exponent, out, raw, powers, tile, upper, lower, acc_a, acc_b, sums, direct, mirror,
           load_sem, power_sem, plane_send, plane_recv, up_send, up_recv, down_send, down_recv, extra_send,
           direct_send, direct_recv, mirror_send, mirror_recv):
    z, c, d = lax.axis_index("row"), lax.axis_index("col"), lax.axis_index("depth")
    n, features = raw.shape
    size = n * cols
    half = features // 2
    widths = [half * piece // sum(PIECES) for piece in PIECES]
    starts = [sum(widths[:i]) for i in range(CHUNKS)]
    q = c * depths + d

    def load(half_index, i):
        piece = pl.ds(half_index * half + starts[i], widths[i])
        return pltpu.make_async_copy(mantissa.at[:, piece], raw.at[:, piece], load_sem.at[half_index, i])

    for i in range(CHUNKS):
        for half_index in range(2):
            load(half_index, i).start()
    load_powers = pltpu.make_async_copy(exponent, powers, power_sem)
    load_powers.start()

    barrier = pltpu.get_barrier_semaphore()

    for k in range(cols):
        for kk in range(depths):
            if k or kk:
                there = {"col": c ^ k, "depth": lax.rem(d + kk, depths)}
                pl.semaphore_signal(barrier, inc=1, device_id=there, device_id_type=MESH)

    @pl.when((z > 0) & (z < rows - 1))
    def _():
        pl.semaphore_signal(barrier, inc=1, device_id={"row": z - 1}, device_id_type=MESH)
        pl.semaphore_signal(barrier, inc=1, device_id={"row": z + 1}, device_id_type=MESH)

    load_powers.wait()
    wide = jnp.broadcast_to(powers[...].reshape(1, n), (n, n))
    eye = lax.broadcasted_iota(jnp.int32, (n, n), 0) == lax.broadcasted_iota(jnp.int32, (n, n), 1)
    scale = scale_of(jnp.sum(jnp.where(eye, wide, 0), axis=1, keepdims=True))
    own_rows = pl.ds(pl.multiple_of(c * n, n), n)

    def scaled(half_index, i, block):
        load(half_index, i).wait()
        piece = pl.ds(half_index * half + starts[i], widths[i])
        value = (raw[:, piece].astype(jnp.float32) * scale).astype(jnp.bfloat16)
        tile[own_rows, piece] = value
        block[pl.ds(0, n), pl.ds(starts[i], widths[i])] = value

    per_span = CHUNKS // PLANE

    def plane_block(rel, t):
        first = t // 2 * per_span
        columns = pl.ds(t % 2 * half + starts[first], sum(widths[first : first + per_span]))
        return tile.at[pl.ds(pl.multiple_of((c ^ rel) * n, n), n), columns]

    def plane_copy(rel, bit, t):
        block = plane_block(rel, t)
        return pltpu.make_async_remote_copy(
            src_ref=block, dst_ref=block, send_sem=plane_send.at[rel | bit],
            recv_sem=plane_recv.at[rel | bit, t], device_id={"col": c ^ bit}, device_id_type=MESH)

    def lower_bits(rel):
        bit = (rel & -rel if rel else cols) >> 1
        while bit:
            yield bit
            bit >>= 1

    def plane_arrivals(t):
        for bit in reversed(range(cols.bit_length() - 1)):
            for rel in range(1 << bit, cols, 1 << (bit + 1)):
                block = plane_block(rel, t)
                pltpu.make_async_copy(block, block, plane_recv.at[rel, t]).wait()
                for low in lower_bits(rel):
                    plane_copy(rel, low, t).start()

    def line_copy(buffer, send, recv, there, b, i):
        piece = pl.ds(starts[i], widths[i])
        return pltpu.make_async_remote_copy(
            src_ref=buffer.at[pl.ds(b * n, n), piece], dst_ref=buffer.at[pl.ds((b + 1) * n, n), piece],
            send_sem=send.at[b], recv_sem=recv.at[b + 1, i], device_id={"row": there}, device_id_type=MESH)

    def extra_copy(buffer, recv, there, i):
        piece = pl.ds(starts[i], widths[i])
        return pltpu.make_async_remote_copy(
            src_ref=buffer.at[pl.ds(0, n), piece], dst_ref=buffer.at[pl.ds((rows - 1) * n, n), piece],
            send_sem=extra_send, recv_sem=recv.at[rows - 1, i], device_id={"row": there}, device_id_type=MESH)

    def line_arrived(buffer, recv, b, i):
        block = buffer.at[pl.ds(b * n, n), pl.ds(starts[i], widths[i])]
        pltpu.make_async_copy(block, block, recv.at[b, i]).wait()

    m = rows - 1 - z

    def line_sends(t):
        b, i = divmod(t, CHUNKS)

        @pl.when((z < rows - 2) & (b <= z))
        def _():
            line_copy(upper, up_send, up_recv, z + 1, b, i).start()

        @pl.when((m < rows - 2) & (b <= m))
        def _():
            line_copy(lower, down_send, down_recv, z - 1, b, i).start()

        if b == 1:
            @pl.when(z == 0)
            def _():
                extra_copy(lower, down_recv, z + 1, i).start()

            @pl.when(m == 0)
            def _():
                extra_copy(upper, up_recv, z - 1, i).start()

    def line_arrivals(t):
        b, i = divmod(t, CHUNKS)
        b += 1

        @pl.when(z == rows - 2)
        def _():
            if t == 0:
                line_arrived(lower, down_recv, b, i)
            line_arrived(upper, up_recv, b, i)
            line_copy(upper, up_send, up_recv, z + 1, b, i).start()
            if b == 1 and t:
                line_arrived(lower, down_recv, b, i)

        @pl.when(m == rows - 2)
        def _():
            if t == 0:
                line_arrived(upper, up_recv, b, i)
            line_arrived(lower, down_recv, b, i)
            line_copy(lower, down_send, down_recv, z - 1, b, i).start()
            if b == 1 and t:
                line_arrived(upper, up_recv, b, i)

        @pl.when((z > 1) & (b <= z) & (z < rows - 2))
        def _():
            line_arrived(upper, up_recv, b, i)

        @pl.when((m > 1) & (b <= m) & (m < rows - 2))
        def _():
            line_arrived(lower, down_recv, b, i)

    def last_arrivals(i):
        @pl.when(z == rows - 2)
        def _():
            line_arrived(upper, up_recv, rows - 1, i)

        @pl.when(m == rows - 2)
        def _():
            line_arrived(lower, down_recv, rows - 1, i)

        @pl.when(z == rows - 1)
        def _():
            for b in range(2, rows):
                line_arrived(upper, up_recv, b, i)

        @pl.when(m == rows - 1)
        def _():
            for b in range(2, rows):
                line_arrived(lower, down_recv, b, i)

    dims = (((1,), (1,)), ((), ()))

    def multiply(i):
        piece, other = pl.ds(starts[i], widths[i]), pl.ds(half + starts[i], widths[i])
        term_a = lax.dot_general(upper[:, piece], tile[:, piece], dims, preferred_element_type=jnp.float32)
        term_b = lax.dot_general(lower[:, piece], tile[:, other], dims, preferred_element_type=jnp.float32)
        if i == 0:
            acc_a[...] = term_a
            acc_b[...] = term_b
        else:
            acc_a[...] += term_a
            acc_b[...] += term_b

    line_steps = (rows - 2) * CHUNKS
    plane_done = 0
    for step in range(line_steps + LAG):
        if step < CHUNKS:
            scaled(0, step, upper)
            scaled(1, step, lower)
        if step == 0:
            pl.semaphore_wait(barrier, cols * depths + jnp.where((z >= 2) & (z <= rows - 3), 1, 0))
        if step < line_steps:
            line_sends(step)
        if step < CHUNKS and step % per_span == per_span - 1:
            for t in (step // per_span * 2, step // per_span * 2 + 1):
                for bit in lower_bits(0):
                    plane_copy(0, bit, t).start()
        done = step - LAG
        if done >= 0:
            line_arrivals(done)
            i = done - (rows - 3) * CHUNKS
            due = min((done + 1) // per_span, 2 * PLANE)
            if i >= 0:
                due = max(due, i // per_span * 2 + 2)
            for t in range(plane_done, due):
                plane_arrivals(t)
            plane_done = due
            if i >= 0:
                @pl.when((z == 0) | (m == 0))
                def _():
                    last_arrivals(i)
                    multiply(i)

    @pl.when((z > 0) & (m > 0))
    def _():
        for i in range(CHUNKS):
            last_arrivals(i)
            multiply(i)

    def place(row, tile_index):
        return {"row": row, "col": tile_index // depths, "depth": tile_index % depths}

    stripe = pl.ds(pl.multiple_of(c * n, n), n)

    def direct_copy(b, j):
        return pltpu.make_async_remote_copy(
            src_ref=sums.at[b], dst_ref=direct.at[d, stripe], send_sem=direct_send.at[b],
            recv_sem=direct_recv, device_id=place(z, j), device_id_type=MESH)

    def mirror_copy(b, j):
        return pltpu.make_async_remote_copy(
            src_ref=sums.at[b], dst_ref=mirror.at[d, stripe], send_sem=mirror_send.at[b],
            recv_sem=mirror_recv, device_id=place(j, z), device_id_type=MESH)


    for b in reversed(range(1, rows)):
        j = lax.rem(z - b + rows, rows)

        @pl.when(worked(rows, z, b))
        def _():
            first = jnp.where(held_upper(rows, z, b), acc_a[pl.ds(b * n, n), :], 0.0)
            second = jnp.where(held_lower(rows, z, rows - b), acc_b[pl.ds((rows - b) * n, n), :], 0.0)
            sums[b] = first + second
            mirror_copy(b, j).start()

    sums[0] = acc_a[pl.ds(0, n), :] + acc_b[pl.ds(0, n), :]

    @pl.when(z != q)
    def _():
        mirror_copy(0, z).start()

    @pl.when(z == q)
    def _():
        mirror[d, stripe] = sums[0]

    for b in range(1, rows):
        j = lax.rem(z - b + rows, rows)

        @pl.when(worked(rows, z, b) & (j != q))
        def _():
            direct_copy(b, j).start()

        @pl.when(worked(rows, z, b) & (j == q))
        def _():
            direct[d, stripe] = sums[b]

    def sent(block, sem):
        pltpu.make_async_copy(block, block, sem).wait()

    for b in range(rows - 1):
        @pl.when((b <= z) & (z < rows - 1) & jnp.logical_not((b == 0) & (z == rows - 2)))
        def _():
            sent(upper.at[pl.ds(b * n, n)], up_send.at[b])

        @pl.when((b <= m) & (m < rows - 1) & jnp.logical_not((b == 0) & (m == rows - 2)))
        def _():
            sent(lower.at[pl.ds(b * n, n)], down_send.at[b])

    @pl.when((z == 0) | (m == 0))
    def _():
        sent(upper.at[pl.ds(0, n)], extra_send)

    for rel in range(1, cols):
        sent(tile.at[own_rows], plane_send.at[rel])

    def received(buffer, recv, own):
        @pl.when(own)
        def _():
            others = sums.at[pl.ds(0, cols * depths - 1)]
            pltpu.make_async_copy(others, others, recv).wait()

        @pl.when(jnp.logical_not(own))
        def _():
            pltpu.make_async_copy(buffer, buffer, recv).wait()

    has_direct = (z != q) & worked(rows, z, lax.rem(z - q + rows, rows))
    has_mirror = (z == q) | worked(rows, q, lax.rem(q - z + rows, rows))

    def gathered(buffer):
        total = buffer[0]
        for dd in range(1, depths):
            total = total + buffer[dd]
        return total

    @pl.when(has_direct)
    def _():
        others = sums.at[pl.ds(0, cols * depths - 1)]
        pltpu.make_async_copy(others, others, direct_recv).wait()
        out[...] = gathered(direct).T

    @pl.when(has_mirror)
    def _():
        received(mirror, mirror_recv, z == q)
        total = gathered(mirror)

        @pl.when(has_direct)
        def _():
            out[...] += total

        @pl.when(jnp.logical_not(has_direct))
        def _():
            out[...] = total

    for b in range(rows):
        j = lax.rem(z - b + rows, rows)
        if b:
            @pl.when(worked(rows, z, b))
            def _():
                mirror_copy(b, j).wait_send()

                @pl.when(j != q)
                def _():
                    direct_copy(b, j).wait_send()
        else:
            @pl.when(z != q)
            def _():
                mirror_copy(0, z).wait_send()


def shards(rows, cols, depths, mantissa, exponent):
    n, features = mantissa.shape
    size = n * cols
    half = features // 2
    dma = pltpu.SemaphoreType.DMA
    return pl.pallas_call(
        functools.partial(kernel, rows, cols, depths),
        out_shape=jax.ShapeDtypeStruct((size, size), jnp.float32),
        in_specs=[pl.BlockSpec(memory_space=pltpu.HBM)] * 2,
        out_specs=pl.BlockSpec(memory_space=pltpu.VMEM),
        scratch_shapes=[
            pltpu.VMEM((n, features), jnp.bfloat16),
            pltpu.VMEM((n,), jnp.int32),
            pltpu.VMEM((size, features), jnp.bfloat16),
            pltpu.VMEM((rows * n, half), jnp.bfloat16),
            pltpu.VMEM((rows * n, half), jnp.bfloat16),
            pltpu.VMEM((rows * n, size), jnp.float32),
            pltpu.VMEM((rows * n, size), jnp.float32),
            pltpu.VMEM((rows, n, size), jnp.float32),
            pltpu.VMEM((depths, size, size), jnp.float32),
            pltpu.VMEM((depths, size, size), jnp.float32),
            dma((2, CHUNKS)), dma,
            dma((cols,)), dma((cols, 2 * PLANE)),
            dma((rows,)), dma((rows, CHUNKS)),
            dma((rows,)), dma((rows, CHUNKS)),
            dma,
            dma((rows,)), dma,
            dma((rows,)), dma,
        ],
        compiler_params=pltpu.CompilerParams(
            collective_id=0, has_side_effects=True, vmem_limit_bytes=63 * 2**20),
    )(mantissa, exponent)


def solution(mesh):
    rows, cols, depths = (mesh.shape[axis] for axis in ("row", "col", "depth"))
    assert rows >= 4 and cols & (cols - 1) == 0 and rows == cols * depths
    in_specs = (P(("groups", "row", "col"), "depth"), P(("groups", "row", "col")))
    out_specs = P(("groups", "row"), ("col", "depth"))
    return jax.shard_map(
        functools.partial(shards, rows, cols, depths), mesh=mesh, in_specs=in_specs, out_specs=out_specs, check_vma=False)
```

```python
import functools

import jax
import jax.numpy as jnp
from jax import lax
from jax.experimental import pallas as pl
from jax.experimental.pallas import tpu as pltpu
from jax.sharding import PartitionSpec as P

PIECES = (4, 4, 4, 4)
CHUNKS = len(PIECES)
PLANE = 2
LAG = 3
LAST = CHUNKS - 1
MESH = pl.DeviceIdType.MESH


def held_upper(rows, z, b):
    ordinary = (b >= 1) & (b <= z) & jnp.logical_not((z == rows - 1) & (b == 1))
    return ordinary | ((z == rows - 2) & (b == rows - 1))


def held_lower(rows, z, b):
    return held_upper(rows, rows - 1 - z, b)


def worked(rows, z, b):
    return held_upper(rows, z, b) | held_lower(rows, z, rows - b)


def scale_of(exponent):
    size = jnp.abs(exponent)
    up = jnp.ones(exponent.shape, jnp.float32)
    down = up
    for bit in range(7):
        is_set = ((size >> bit) & 1) == 1
        up = jnp.where(is_set, up * 2.0 ** (2**bit), up)
        down = jnp.where(is_set, down * 2.0 ** -(2**bit), down)
    return jnp.where(exponent < 0, down, up)


def kernel(rows, cols, depths, mantissa, exponent, out, raw, powers, tile, upper, lower, acc_a, acc_b, sums, direct, mirror,
           load_sem, power_sem, plane_send, plane_recv, up_send, up_recv, down_send, down_recv, extra_send, beyond_send,
           direct_send, direct_recv, mirror_send, mirror_recv):
    z, c, d = lax.axis_index("row"), lax.axis_index("col"), lax.axis_index("depth")
    n, features = raw.shape
    size = n * cols
    half = features // 2
    widths = [half * piece // sum(PIECES) for piece in PIECES]
    starts = [sum(widths[:i]) for i in range(CHUNKS)]
    q = c * depths + d

    def load(half_index, i):
        piece = pl.ds(half_index * half + starts[i], widths[i])
        return pltpu.make_async_copy(mantissa.at[:, piece], raw.at[:, piece], load_sem.at[half_index, i])

    for i in range(CHUNKS):
        for half_index in range(2):
            load(half_index, i).start()
    load_powers = pltpu.make_async_copy(exponent, powers, power_sem)
    load_powers.start()

    barrier = pltpu.get_barrier_semaphore()

    for k in range(cols):
        for kk in range(depths):
            if k or kk:
                there = {"col": c ^ k, "depth": lax.rem(d + kk, depths)}
                pl.semaphore_signal(barrier, inc=1, device_id=there, device_id_type=MESH)

    @pl.when((z > 0) & (z < rows - 1))
    def _():
        pl.semaphore_signal(barrier, inc=1, device_id={"row": z - 1}, device_id_type=MESH)
        pl.semaphore_signal(barrier, inc=1, device_id={"row": z + 1}, device_id_type=MESH)

    load_powers.wait()
    wide = jnp.broadcast_to(powers[...].reshape(1, n), (n, n))
    eye = lax.broadcasted_iota(jnp.int32, (n, n), 0) == lax.broadcasted_iota(jnp.int32, (n, n), 1)
    scale = scale_of(jnp.sum(jnp.where(eye, wide, 0), axis=1, keepdims=True))
    own_rows = pl.ds(pl.multiple_of(c * n, n), n)

    def scaled(half_index, i, block):
        load(half_index, i).wait()
        piece = pl.ds(half_index * half + starts[i], widths[i])
        value = (raw[:, piece].astype(jnp.float32) * scale).astype(jnp.bfloat16)
        tile[own_rows, piece] = value
        block[pl.ds(0, n), pl.ds(starts[i], widths[i])] = value

    per_span = CHUNKS // PLANE

    def plane_block(rel, t):
        first = t // 2 * per_span
        columns = pl.ds(t % 2 * half + starts[first], sum(widths[first : first + per_span]))
        return tile.at[pl.ds(pl.multiple_of((c ^ rel) * n, n), n), columns]

    def plane_copy(rel, bit, t):
        block = plane_block(rel, t)
        return pltpu.make_async_remote_copy(
            src_ref=block, dst_ref=block, send_sem=plane_send.at[rel | bit],
            recv_sem=plane_recv.at[rel | bit, t], device_id={"col": c ^ bit}, device_id_type=MESH)

    def lower_bits(rel):
        bit = (rel & -rel if rel else cols) >> 1
        while bit:
            yield bit
            bit >>= 1

    def plane_arrivals(t):
        for bit in reversed(range(cols.bit_length() - 1)):
            for rel in range(1 << bit, cols, 1 << (bit + 1)):
                block = plane_block(rel, t)
                pltpu.make_async_copy(block, block, plane_recv.at[rel, t]).wait()
                for low in lower_bits(rel):
                    plane_copy(rel, low, t).start()

    def line_copy(buffer, send, recv, there, b, i):
        piece = pl.ds(starts[i], widths[i])
        return pltpu.make_async_remote_copy(
            src_ref=buffer.at[pl.ds(b * n, n), piece], dst_ref=buffer.at[pl.ds((b + 1) * n, n), piece],
            send_sem=send.at[b], recv_sem=recv.at[b + 1, i], device_id={"row": there}, device_id_type=MESH)

    def extra_copy(buffer, recv, there, i):
        piece = pl.ds(starts[i], widths[i])
        return pltpu.make_async_remote_copy(
            src_ref=buffer.at[pl.ds(0, n), piece], dst_ref=buffer.at[pl.ds((rows - 1) * n, n), piece],
            send_sem=extra_send, recv_sem=recv.at[rows - 1, i], device_id={"row": there}, device_id_type=MESH)

    def line_arrived(buffer, recv, b, i):
        block = buffer.at[pl.ds(b * n, n), pl.ds(starts[i], widths[i])]
        pltpu.make_async_copy(block, block, recv.at[b, i]).wait()

    m = rows - 1 - z

    def line_sends(t):
        b, i = divmod(t, CHUNKS)

        late = t == LAST

        @pl.when((z < rows - 2 - late) & (b <= z))
        def _():
            line_copy(upper, up_send, up_recv, z + 1, b, i).start()

        @pl.when((m < rows - 2 - late) & (b <= m))
        def _():
            line_copy(lower, down_send, down_recv, z - 1, b, i).start()

        if b == 1:
            @pl.when(z == 0)
            def _():
                extra_copy(lower, down_recv, z + 1, (i + LAST) % CHUNKS).start()

            @pl.when(m == 0)
            def _():
                extra_copy(upper, up_recv, z - 1, (i + LAST) % CHUNKS).start()

    def late_sends():
        @pl.when(z == rows - 3)
        def _():
            line_copy(upper, up_send, up_recv, z + 1, 0, LAST).start()

        @pl.when(m == rows - 3)
        def _():
            line_copy(lower, down_send, down_recv, z - 1, 0, LAST).start()

    def beyond_copy(buffer, recv, there):
        piece = pl.ds(starts[LAST], widths[LAST])
        return pltpu.make_async_remote_copy(
            src_ref=buffer.at[pl.ds((rows - 1) * n, n), piece], dst_ref=buffer.at[pl.ds((rows - 2) * n, n), piece],
            send_sem=beyond_send, recv_sem=recv.at[rows - 2, LAST], device_id={"row": there}, device_id_type=MESH)

    def beyond_sends():
        @pl.when(z == 1)
        def _():
            line_arrived(lower, down_recv, rows - 1, LAST)
            beyond_copy(lower, down_recv, z + 1).start()

        @pl.when(m == 1)
        def _():
            line_arrived(upper, up_recv, rows - 1, LAST)
            beyond_copy(upper, up_recv, z - 1).start()

    def line_arrivals(t):
        b, i = divmod(t, CHUNKS)
        b += 1

        @pl.when(z == rows - 2)
        def _():
            if t == 0:
                line_arrived(lower, down_recv, b, i)
            if t != LAST:
                line_arrived(upper, up_recv, b, i)
                line_copy(upper, up_send, up_recv, z + 1, b, i).start()
            if b == 1 and t:
                line_arrived(lower, down_recv, b, i)

        @pl.when(m == rows - 2)
        def _():
            if t == 0:
                line_arrived(upper, up_recv, b, i)
            if t != LAST:
                line_arrived(lower, down_recv, b, i)
                line_copy(lower, down_send, down_recv, z - 1, b, i).start()
            if b == 1 and t:
                line_arrived(upper, up_recv, b, i)

        @pl.when((z > 1) & (b <= z) & (z < rows - 2))
        def _():
            line_arrived(upper, up_recv, b, i)

        @pl.when((m > 1) & (b <= m) & (m < rows - 2))
        def _():
            line_arrived(lower, down_recv, b, i)

    def last_arrivals(i):
        for at, buffer, recv in ((m, upper, up_recv), (z, lower, down_recv)):
            @pl.when(at == 0)
            def _():
                for b in range(3 if i == LAST else 2, rows):
                    line_arrived(buffer, recv, b, i)

            @pl.when(at == 1)
            def _():
                line_arrived(buffer, recv, 1 if i == LAST else rows - 1, i)

            if i == LAST:
                @pl.when(at == 2)
                def _():
                    line_arrived(buffer, recv, rows - 2, i)

    dims = (((1,), (1,)), ((), ()))

    def multiply(i):
        piece, other = pl.ds(starts[i], widths[i]), pl.ds(half + starts[i], widths[i])
        term_a = lax.dot_general(upper[:, piece], tile[:, piece], dims, preferred_element_type=jnp.float32)
        term_b = lax.dot_general(lower[:, piece], tile[:, other], dims, preferred_element_type=jnp.float32)
        block = lax.broadcasted_iota(jnp.int32, (rows * n, size), 0) // n
        if i == LAST:
            term_a = jnp.where((m == 0) & (block == 2), 0.0, term_a)
            term_b = jnp.where((z == 0) & (block == 2), 0.0, term_b)
        else:
            term_a = jnp.where((m == 2) & (block == rows - 2), 0.0, term_a)
            term_b = jnp.where((z == 2) & (block == rows - 2), 0.0, term_b)
        if i == 0:
            acc_a[...] = term_a
            acc_b[...] = term_b
        else:
            acc_a[...] += term_a
            acc_b[...] += term_b

    line_steps = (rows - 2) * CHUNKS
    plane_done = 0
    for step in range(line_steps + LAG):
        if step < CHUNKS:
            scaled(0, step, upper)
            scaled(1, step, lower)
        if step == 0:
            pl.semaphore_wait(barrier, cols * depths + jnp.where((z >= 2) & (z <= rows - 3), 1, 0))
        if step < line_steps:
            line_sends(step)
        if step == line_steps - 1:
            late_sends()
        if step < CHUNKS and step % per_span == per_span - 1:
            for t in (step // per_span * 2, step // per_span * 2 + 1):
                for bit in lower_bits(0):
                    plane_copy(0, bit, t).start()
        done = step - LAG
        if done >= 0:
            line_arrivals(done)
        if step == line_steps:
            beyond_sends()
        if done >= 0:
            i = done - (rows - 3) * CHUNKS
            due = min((done + 1) // per_span, 2 * PLANE)
            if i >= 0:
                due = max(due, i // per_span * 2 + 2)
            for t in range(plane_done, due):
                plane_arrivals(t)
            plane_done = due
            if i >= 0:
                @pl.when((z == 0) | (m == 0))
                def _():
                    last_arrivals(i)
                    multiply(i)

    @pl.when((z > 0) & (m > 0))
    def _():
        for i in range(CHUNKS):
            last_arrivals(i)
            multiply(i)

    def place(row, tile_index):
        return {"row": row, "col": tile_index // depths, "depth": tile_index % depths}

    stripe = pl.ds(pl.multiple_of(c * n, n), n)

    def direct_copy(b, j):
        return pltpu.make_async_remote_copy(
            src_ref=sums.at[b], dst_ref=direct.at[d, stripe], send_sem=direct_send.at[b],
            recv_sem=direct_recv, device_id=place(z, j), device_id_type=MESH)

    def mirror_copy(b, j):
        return pltpu.make_async_remote_copy(
            src_ref=sums.at[b], dst_ref=mirror.at[d, stripe], send_sem=mirror_send.at[b],
            recv_sem=mirror_recv, device_id=place(j, z), device_id_type=MESH)


    for b in reversed(range(1, rows)):
        j = lax.rem(z - b + rows, rows)

        @pl.when(worked(rows, z, b))
        def _():
            first = jnp.where(held_upper(rows, z, b) | ((m == 2) & (b == rows - 2)), acc_a[pl.ds(b * n, n), :], 0.0)
            second = jnp.where(held_lower(rows, z, rows - b) | ((z == 2) & (b == 2)), acc_b[pl.ds((rows - b) * n, n), :], 0.0)
            sums[b] = first + second
            mirror_copy(b, j).start()

    sums[0] = acc_a[pl.ds(0, n), :] + acc_b[pl.ds(0, n), :]

    @pl.when(z != q)
    def _():
        mirror_copy(0, z).start()

    @pl.when(z == q)
    def _():
        mirror[d, stripe] = sums[0]

    for b in range(1, rows):
        j = lax.rem(z - b + rows, rows)

        @pl.when(worked(rows, z, b) & (j != q))
        def _():
            direct_copy(b, j).start()

        @pl.when(worked(rows, z, b) & (j == q))
        def _():
            direct[d, stripe] = sums[b]

    def sent(block, sem):
        pltpu.make_async_copy(block, block, sem).wait()

    for b in range(rows - 1):
        for at, buffer, send in ((z, upper, up_send), (m, lower, down_send)):
            @pl.when((b <= at) & (at < rows - 2))
            def _():
                sent(buffer.at[pl.ds(b * n, n)], send.at[b])

            if b:
                @pl.when(at == rows - 2)
                def _():
                    sent(buffer.at[pl.ds(b * n, n), pl.ds(0, starts[LAST] if b == 1 else half)], send.at[b])

    @pl.when((z == 1) | (m == 1))
    def _():
        sent(upper.at[pl.ds(0, n), pl.ds(starts[LAST], widths[LAST])], beyond_send)

    @pl.when((z == 0) | (m == 0))
    def _():
        sent(upper.at[pl.ds(0, n)], extra_send)

    for rel in range(1, cols):
        sent(tile.at[own_rows], plane_send.at[rel])

    def received(buffer, recv, own):
        @pl.when(own)
        def _():
            others = sums.at[pl.ds(0, cols * depths - 1)]
            pltpu.make_async_copy(others, others, recv).wait()

        @pl.when(jnp.logical_not(own))
        def _():
            pltpu.make_async_copy(buffer, buffer, recv).wait()

    has_direct = (z != q) & worked(rows, z, lax.rem(z - q + rows, rows))
    has_mirror = (z == q) | worked(rows, q, lax.rem(q - z + rows, rows))

    def gathered(buffer):
        total = buffer[0]
        for dd in range(1, depths):
            total = total + buffer[dd]
        return total

    @pl.when(has_direct)
    def _():
        others = sums.at[pl.ds(0, cols * depths - 1)]
        pltpu.make_async_copy(others, others, direct_recv).wait()
        out[...] = gathered(direct).T

    @pl.when(has_mirror)
    def _():
        received(mirror, mirror_recv, z == q)
        total = gathered(mirror)

        @pl.when(has_direct)
        def _():
            out[...] += total

        @pl.when(jnp.logical_not(has_direct))
        def _():
            out[...] = total

    for b in range(rows):
        j = lax.rem(z - b + rows, rows)
        if b:
            @pl.when(worked(rows, z, b))
            def _():
                mirror_copy(b, j).wait_send()

                @pl.when(j != q)
                def _():
                    direct_copy(b, j).wait_send()
        else:
            @pl.when(z != q)
            def _():
                mirror_copy(0, z).wait_send()


def shards(rows, cols, depths, mantissa, exponent):
    n, features = mantissa.shape
    size = n * cols
    half = features // 2
    dma = pltpu.SemaphoreType.DMA
    return pl.pallas_call(
        functools.partial(kernel, rows, cols, depths),
        out_shape=jax.ShapeDtypeStruct((size, size), jnp.float32),
        in_specs=[pl.BlockSpec(memory_space=pltpu.HBM)] * 2,
        out_specs=pl.BlockSpec(memory_space=pltpu.VMEM),
        scratch_shapes=[
            pltpu.VMEM((n, features), jnp.bfloat16),
            pltpu.VMEM((n,), jnp.int32),
            pltpu.VMEM((size, features), jnp.bfloat16),
            pltpu.VMEM((rows * n, half), jnp.bfloat16),
            pltpu.VMEM((rows * n, half), jnp.bfloat16),
            pltpu.VMEM((rows * n, size), jnp.float32),
            pltpu.VMEM((rows * n, size), jnp.float32),
            pltpu.VMEM((rows, n, size), jnp.float32),
            pltpu.VMEM((depths, size, size), jnp.float32),
            pltpu.VMEM((depths, size, size), jnp.float32),
            dma((2, CHUNKS)), dma,
            dma((cols,)), dma((cols, 2 * PLANE)),
            dma((rows,)), dma((rows, CHUNKS)),
            dma((rows,)), dma((rows, CHUNKS)),
            dma, dma,
            dma((rows,)), dma,
            dma((rows,)), dma,
        ],
        compiler_params=pltpu.CompilerParams(
            collective_id=0, has_side_effects=True, vmem_limit_bytes=63 * 2**20),
    )(mantissa, exponent)


def solution(mesh):
    rows, cols, depths = (mesh.shape[axis] for axis in ("row", "col", "depth"))
    assert rows >= 4 and cols & (cols - 1) == 0 and rows == cols * depths
    in_specs = (P(("groups", "row", "col"), "depth"), P(("groups", "row", "col")))
    out_specs = P(("groups", "row"), ("col", "depth"))
    return jax.shard_map(
        functools.partial(shards, rows, cols, depths), mesh=mesh, in_specs=in_specs, out_specs=out_specs, check_vma=False)
```

```python
import functools

import jax
import jax.numpy as jnp
from jax import lax
from jax.experimental import pallas as pl
from jax.experimental.pallas import tpu as pltpu
from jax.sharding import PartitionSpec as P

PIECES = (4, 4, 4, 4)
CHUNKS = len(PIECES)
PLANE = 2
LAG = 3
LAST = CHUNKS - 1
MESH = pl.DeviceIdType.MESH


def held_upper(rows, z, b):
    ordinary = (b >= 1) & (b <= z) & jnp.logical_not((z == rows - 1) & (b == 1))
    return ordinary | ((z == rows - 2) & (b == rows - 1))


def held_lower(rows, z, b):
    return held_upper(rows, rows - 1 - z, b)


def worked(rows, z, b):
    return held_upper(rows, z, b) | held_lower(rows, z, rows - b)


def scale_of(exponent):
    size = jnp.abs(exponent)
    up = jnp.ones(exponent.shape, jnp.float32)
    down = up
    for bit in range(7):
        is_set = ((size >> bit) & 1) == 1
        up = jnp.where(is_set, up * 2.0 ** (2**bit), up)
        down = jnp.where(is_set, down * 2.0 ** -(2**bit), down)
    return jnp.where(exponent < 0, down, up)


def kernel(rows, cols, depths, mantissa, exponent, out, raw, powers, tile, upper, lower, acc_a, acc_b, sums, direct, mirror,
           load_sem, power_sem, plane_send, plane_recv, up_send, up_recv, down_send, down_recv, extra_send, beyond_send,
           direct_send, direct_recv, mirror_send, mirror_recv):
    z, c, d = lax.axis_index("row"), lax.axis_index("col"), lax.axis_index("depth")
    n, features = raw.shape
    size = n * cols
    half = features // 2
    widths = [half * piece // sum(PIECES) for piece in PIECES]
    starts = [sum(widths[:i]) for i in range(CHUNKS)]
    q = c * depths + d

    def load(half_index, i):
        piece = pl.ds(half_index * half + starts[i], widths[i])
        return pltpu.make_async_copy(mantissa.at[:, piece], raw.at[:, piece], load_sem.at[half_index, i])

    for i in range(CHUNKS):
        for half_index in range(2):
            load(half_index, i).start()
    load_powers = pltpu.make_async_copy(exponent, powers, power_sem)
    load_powers.start()

    barrier = pltpu.get_barrier_semaphore()

    for k in range(cols):
        for kk in range(depths):
            if k or kk:
                there = {"col": c ^ k, "depth": lax.rem(d + kk, depths)}
                pl.semaphore_signal(barrier, inc=1, device_id=there, device_id_type=MESH)

    @pl.when((z > 0) & (z < rows - 1))
    def _():
        pl.semaphore_signal(barrier, inc=1, device_id={"row": z - 1}, device_id_type=MESH)
        pl.semaphore_signal(barrier, inc=1, device_id={"row": z + 1}, device_id_type=MESH)

    load_powers.wait()
    wide = jnp.broadcast_to(powers[...].reshape(1, n), (n, n))
    eye = lax.broadcasted_iota(jnp.int32, (n, n), 0) == lax.broadcasted_iota(jnp.int32, (n, n), 1)
    scale = scale_of(jnp.sum(jnp.where(eye, wide, 0), axis=1, keepdims=True))
    own_rows = pl.ds(pl.multiple_of(c * n, n), n)

    def scaled(half_index, i, block):
        load(half_index, i).wait()
        piece = pl.ds(half_index * half + starts[i], widths[i])
        value = (raw[:, piece].astype(jnp.float32) * scale).astype(jnp.bfloat16)
        tile[own_rows, piece] = value
        block[pl.ds(0, n), pl.ds(starts[i], widths[i])] = value

    per_span = CHUNKS // PLANE
    span = half // PLANE

    def plane_block(rel, t):
        upper_first, lower_first = t * span, (t + PLANE) % (2 * PLANE) * span
        by_turns = t % 2 * half + t // 2 * span
        start = jnp.where(z == 0, lower_first, jnp.where(z == rows - 1, upper_first, by_turns))
        columns = pl.ds(pl.multiple_of(start, span), span)
        return tile.at[pl.ds(pl.multiple_of((c ^ rel) * n, n), n), columns]

    def plane_copy(rel, bit, t):
        block = plane_block(rel, t)
        return pltpu.make_async_remote_copy(
            src_ref=block, dst_ref=block, send_sem=plane_send.at[rel | bit],
            recv_sem=plane_recv.at[rel | bit, t], device_id={"col": c ^ bit}, device_id_type=MESH)

    def lower_bits(rel):
        bit = (rel & -rel if rel else cols) >> 1
        while bit:
            yield bit
            bit >>= 1

    def plane_wait(rel, t):
        block = plane_block(rel, t)
        pltpu.make_async_copy(block, block, plane_recv.at[rel, t]).wait()

    def plane_pass(t):
        for bit in reversed(range(1, cols.bit_length() - 1)):
            for rel in range(1 << bit, cols, 1 << (bit + 1)):
                plane_wait(rel, t)
                for low in lower_bits(rel):
                    plane_copy(rel, low, t).start()

    def plane_rest(t):
        for rel in range(1, cols, 2):
            plane_wait(rel, t)

    def line_copy(buffer, send, recv, there, b, i):
        piece = pl.ds(starts[i], widths[i])
        return pltpu.make_async_remote_copy(
            src_ref=buffer.at[pl.ds(b * n, n), piece], dst_ref=buffer.at[pl.ds((b + 1) * n, n), piece],
            send_sem=send.at[b], recv_sem=recv.at[b + 1, i], device_id={"row": there}, device_id_type=MESH)

    def extra_copy(buffer, recv, there, i):
        piece = pl.ds(starts[i], widths[i])
        return pltpu.make_async_remote_copy(
            src_ref=buffer.at[pl.ds(0, n), piece], dst_ref=buffer.at[pl.ds((rows - 1) * n, n), piece],
            send_sem=extra_send, recv_sem=recv.at[rows - 1, i], device_id={"row": there}, device_id_type=MESH)

    def line_arrived(buffer, recv, b, i):
        block = buffer.at[pl.ds(b * n, n), pl.ds(starts[i], widths[i])]
        pltpu.make_async_copy(block, block, recv.at[b, i]).wait()

    m = rows - 1 - z

    def line_sends(t):
        b, i = divmod(t, CHUNKS)

        late = t == LAST

        @pl.when((z < rows - 2 - late) & (b <= z))
        def _():
            line_copy(upper, up_send, up_recv, z + 1, b, i).start()

        @pl.when((m < rows - 2 - late) & (b <= m))
        def _():
            line_copy(lower, down_send, down_recv, z - 1, b, i).start()

        if b == 1:
            @pl.when(z == 0)
            def _():
                extra_copy(lower, down_recv, z + 1, (i + LAST) % CHUNKS).start()

            @pl.when(m == 0)
            def _():
                extra_copy(upper, up_recv, z - 1, (i + LAST) % CHUNKS).start()

    def late_sends():
        @pl.when(z == rows - 3)
        def _():
            line_copy(upper, up_send, up_recv, z + 1, 0, LAST).start()

        @pl.when(m == rows - 3)
        def _():
            line_copy(lower, down_send, down_recv, z - 1, 0, LAST).start()

    def beyond_copy(buffer, recv, there):
        piece = pl.ds(starts[LAST], widths[LAST])
        return pltpu.make_async_remote_copy(
            src_ref=buffer.at[pl.ds((rows - 1) * n, n), piece], dst_ref=buffer.at[pl.ds((rows - 2) * n, n), piece],
            send_sem=beyond_send, recv_sem=recv.at[rows - 2, LAST], device_id={"row": there}, device_id_type=MESH)

    def beyond_sends():
        @pl.when(z == 1)
        def _():
            line_arrived(lower, down_recv, rows - 1, LAST)
            beyond_copy(lower, down_recv, z + 1).start()

        @pl.when(m == 1)
        def _():
            line_arrived(upper, up_recv, rows - 1, LAST)
            beyond_copy(upper, up_recv, z - 1).start()

    def line_arrivals(t):
        b, i = divmod(t, CHUNKS)
        b += 1

        @pl.when(z == rows - 2)
        def _():
            if t == 0:
                line_arrived(lower, down_recv, b, i)
            if t != LAST:
                line_arrived(upper, up_recv, b, i)
                line_copy(upper, up_send, up_recv, z + 1, b, i).start()
            if b == 1 and t:
                line_arrived(lower, down_recv, b, i)

        @pl.when(m == rows - 2)
        def _():
            if t == 0:
                line_arrived(upper, up_recv, b, i)
            if t != LAST:
                line_arrived(lower, down_recv, b, i)
                line_copy(lower, down_send, down_recv, z - 1, b, i).start()
            if b == 1 and t:
                line_arrived(upper, up_recv, b, i)

        @pl.when((z > 1) & (b <= z) & (z < rows - 2))
        def _():
            line_arrived(upper, up_recv, b, i)

        @pl.when((m > 1) & (b <= m) & (m < rows - 2))
        def _():
            line_arrived(lower, down_recv, b, i)

    def last_arrivals(i):
        for at, buffer, recv in ((m, upper, up_recv), (z, lower, down_recv)):
            @pl.when(at == 0)
            def _():
                for b in range(3 if i == LAST else 2, rows):
                    line_arrived(buffer, recv, b, i)

            @pl.when(at == 1)
            def _():
                line_arrived(buffer, recv, 1 if i == LAST else rows - 1, i)

            if i == LAST:
                @pl.when(at == 2)
                def _():
                    line_arrived(buffer, recv, rows - 2, i)

    dims = (((1,), (1,)), ((), ()))

    block = lax.broadcasted_iota(jnp.int32, (rows * n, size), 0) // n

    def add(acc, features_of, offset, at, i):
        term = lax.dot_general(
            features_of[:, pl.ds(starts[i], widths[i])], tile[:, pl.ds(offset + starts[i], widths[i])], dims,
            preferred_element_type=jnp.float32)
        if i == LAST:
            term = jnp.where((at == 0) & (block == 2), 0.0, term)
        else:
            term = jnp.where((at == 2) & (block == rows - 2), 0.0, term)
        if i == 0:
            acc[...] = term
        else:
            acc[...] += term

    def multiply_upper(i):
        add(acc_a, upper, 0, m, i)

    def multiply_lower(i):
        add(acc_b, lower, half, z, i)

    line_steps = (rows - 2) * CHUNKS
    plane_done = 0
    for step in range(line_steps + LAG):
        if step < CHUNKS:
            scaled(0, step, upper)
            scaled(1, step, lower)
        if step == 0:
            pl.semaphore_wait(barrier, cols * depths + jnp.where((z >= 2) & (z <= rows - 3), 1, 0))
        if step < line_steps:
            line_sends(step)
        if step == line_steps - 1:
            late_sends()
        if step in (per_span - 1, CHUNKS - 1):
            for t in range(1) if step < CHUNKS - 1 else range(1, 2 * PLANE):
                for bit in lower_bits(0):
                    plane_copy(0, bit, t).start()
        done = step - LAG
        if done >= 0:
            line_arrivals(done)
        if step == line_steps:
            beyond_sends()
        if done >= 0:
            due = min((done + 1) // per_span, 2 * PLANE)
            for t in range(plane_done, due):
                plane_pass(t)
            plane_done = due
            i = done - (rows - 3) * CHUNKS
            if i >= 0:
                @pl.when((z == 0) | (m == 0))
                def _():
                    if i % per_span == 0:
                        plane_rest(i // per_span)
                    last_arrivals(i)

                @pl.when(z == 0)
                def _():
                    multiply_lower(i)

                @pl.when(m == 0)
                def _():
                    multiply_upper(i)

    @pl.when((z > 0) & (m > 0))
    def _():
        for t in range(2 * PLANE):
            plane_rest(t)
        for i in range(CHUNKS):
            last_arrivals(i)
            multiply_upper(i)
            multiply_lower(i)

    def place(row, tile_index):
        return {"row": row, "col": tile_index // depths, "depth": tile_index % depths}

    stripe = pl.ds(pl.multiple_of(c * n, n), n)

    def direct_copy(b, j):
        return pltpu.make_async_remote_copy(
            src_ref=sums.at[b], dst_ref=direct.at[d, stripe], send_sem=direct_send.at[b],
            recv_sem=direct_recv, device_id=place(z, j), device_id_type=MESH)

    def mirror_copy(b, j):
        return pltpu.make_async_remote_copy(
            src_ref=sums.at[b], dst_ref=mirror.at[d, stripe], send_sem=mirror_send.at[b],
            recv_sem=mirror_recv, device_id=place(j, z), device_id_type=MESH)


    for b in reversed(range(1, rows)):
        j = lax.rem(z - b + rows, rows)

        @pl.when(worked(rows, z, b))
        def _():
            first = jnp.where(held_upper(rows, z, b) | ((m == 2) & (b == rows - 2)), acc_a[pl.ds(b * n, n), :], 0.0)
            second = jnp.where(held_lower(rows, z, rows - b) | ((z == 2) & (b == 2)), acc_b[pl.ds((rows - b) * n, n), :], 0.0)
            sums[b] = first + second
            mirror_copy(b, j).start()

    for b in range(1, rows):
        j = lax.rem(z - b + rows, rows)

        @pl.when(worked(rows, z, b) & (j != q))
        def _():
            direct_copy(b, j).start()

        @pl.when(worked(rows, z, b) & (j == q))
        def _():
            direct[d, stripe] = sums[b]

    for i in range(CHUNKS):
        @pl.when((z == 0) | (m == 0))
        def _():
            if i % per_span == 0:
                plane_rest(PLANE + i // per_span)

        piece = pl.ds(starts[i], widths[i])
        for at, acc, features_of, offset in ((z, acc_a, upper, 0), (m, acc_b, lower, half)):
            @pl.when(at == 0)
            def _():
                term = lax.dot_general(
                    features_of[pl.ds(0, n), piece], tile[:, pl.ds(offset + starts[i], widths[i])], dims,
                    preferred_element_type=jnp.float32)
                acc[pl.ds(0, n), :] = term if i == 0 else acc[pl.ds(0, n), :] + term

    sums[0] = acc_a[pl.ds(0, n), :] + acc_b[pl.ds(0, n), :]

    @pl.when(z != q)
    def _():
        mirror_copy(0, z).start()

    @pl.when(z == q)
    def _():
        mirror[d, stripe] = sums[0]

    def sent(block, sem):
        pltpu.make_async_copy(block, block, sem).wait()

    for b in range(rows - 1):
        for at, buffer, send in ((z, upper, up_send), (m, lower, down_send)):
            @pl.when((b <= at) & (at < rows - 2))
            def _():
                sent(buffer.at[pl.ds(b * n, n)], send.at[b])

            if b:
                @pl.when(at == rows - 2)
                def _():
                    sent(buffer.at[pl.ds(b * n, n), pl.ds(0, starts[LAST] if b == 1 else half)], send.at[b])

    @pl.when((z == 1) | (m == 1))
    def _():
        sent(upper.at[pl.ds(0, n), pl.ds(starts[LAST], widths[LAST])], beyond_send)

    @pl.when((z == 0) | (m == 0))
    def _():
        sent(upper.at[pl.ds(0, n)], extra_send)

    for rel in range(1, cols):
        sent(tile.at[own_rows], plane_send.at[rel])

    def received(buffer, recv, own):
        @pl.when(own)
        def _():
            others = sums.at[pl.ds(0, cols * depths - 1)]
            pltpu.make_async_copy(others, others, recv).wait()

        @pl.when(jnp.logical_not(own))
        def _():
            pltpu.make_async_copy(buffer, buffer, recv).wait()

    has_direct = (z != q) & worked(rows, z, lax.rem(z - q + rows, rows))
    has_mirror = (z == q) | worked(rows, q, lax.rem(q - z + rows, rows))

    def gathered(buffer):
        total = buffer[0]
        for dd in range(1, depths):
            total = total + buffer[dd]
        return total

    @pl.when(has_direct)
    def _():
        others = sums.at[pl.ds(0, cols * depths - 1)]
        pltpu.make_async_copy(others, others, direct_recv).wait()
        out[...] = gathered(direct).T

    @pl.when(has_mirror)
    def _():
        received(mirror, mirror_recv, z == q)
        total = gathered(mirror)

        @pl.when(has_direct)
        def _():
            out[...] += total

        @pl.when(jnp.logical_not(has_direct))
        def _():
            out[...] = total

    for b in range(rows):
        j = lax.rem(z - b + rows, rows)
        if b:
            @pl.when(worked(rows, z, b))
            def _():
                mirror_copy(b, j).wait_send()

                @pl.when(j != q)
                def _():
                    direct_copy(b, j).wait_send()
        else:
            @pl.when(z != q)
            def _():
                mirror_copy(0, z).wait_send()


def shards(rows, cols, depths, mantissa, exponent):
    n, features = mantissa.shape
    size = n * cols
    half = features // 2
    dma = pltpu.SemaphoreType.DMA
    return pl.pallas_call(
        functools.partial(kernel, rows, cols, depths),
        out_shape=jax.ShapeDtypeStruct((size, size), jnp.float32),
        in_specs=[pl.BlockSpec(memory_space=pltpu.HBM)] * 2,
        out_specs=pl.BlockSpec(memory_space=pltpu.VMEM),
        scratch_shapes=[
            pltpu.VMEM((n, features), jnp.bfloat16),
            pltpu.VMEM((n,), jnp.int32),
            pltpu.VMEM((size, features), jnp.bfloat16),
            pltpu.VMEM((rows * n, half), jnp.bfloat16),
            pltpu.VMEM((rows * n, half), jnp.bfloat16),
            pltpu.VMEM((rows * n, size), jnp.float32),
            pltpu.VMEM((rows * n, size), jnp.float32),
            pltpu.VMEM((rows, n, size), jnp.float32),
            pltpu.VMEM((depths, size, size), jnp.float32),
            pltpu.VMEM((depths, size, size), jnp.float32),
            dma((2, CHUNKS)), dma,
            dma((cols,)), dma((cols, 2 * PLANE)),
            dma((rows,)), dma((rows, CHUNKS)),
            dma((rows,)), dma((rows, CHUNKS)),
            dma, dma,
            dma((rows,)), dma,
            dma((rows,)), dma,
        ],
        compiler_params=pltpu.CompilerParams(
            collective_id=0, has_side_effects=True, vmem_limit_bytes=63 * 2**20),
    )(mantissa, exponent)


def solution(mesh):
    rows, cols, depths = (mesh.shape[axis] for axis in ("row", "col", "depth"))
    assert rows >= 4 and cols & (cols - 1) == 0 and rows == cols * depths
    in_specs = (P(("groups", "row", "col"), "depth"), P(("groups", "row", "col")))
    out_specs = P(("groups", "row"), ("col", "depth"))
    return jax.shard_map(
        functools.partial(shards, rows, cols, depths), mesh=mesh, in_specs=in_specs, out_specs=out_specs, check_vma=False)
```
